1024 devices in a mesh: section: 64 (over z_lo, y, core), dp: 16 (over x, z_hi).
Axes of the slice: x: 4, y: 4, z: 32 (z_hi: 4, z_lo: 8; z = z_hi * 8 + z_lo), core: 2. Of those that a mesh axis runs over, the one named last changes fastest.
Arguments:
- enc_out: bfloat16 [4, 256, 4096], P(None, 'section'), may hold values from -6 to 6
- kv_weight: bfloat16 [2, 4096, 4096], P(None, None, 'dp'), may hold values from -0.09375 to 0.09375
- queries: bfloat16 [64, 1024, 4096], P('section', None, 'dp'), may hold values from -6 to 6
- carried: bfloat16 [64, 1024, 4096], P('section', None, 'dp'), may hold values from -4 to 4
- roster: int32 [64], P('section'), may hold values from 0 to 3
- cotangent: bfloat16 [64, 1024, 4096], P('section', None, 'dp'), may hold values from -6 to 6
Outputs:
- section_out: bfloat16 [64, 1024, 4096], P('section', None, 'dp')
- d_queries: bfloat16 [64, 1024, 4096], P('section', None, 'dp')
- d_enc_out: bfloat16 [4, 256, 4096], P(None, 'section')
- d_kv_weight: float32 [2, 4096, 4096], P(None, 'section', 'dp')
The draws below stay inside these ranges and needn't reach their ends.
All inputs are finite; a program needn't handle non-finite values.
Results may differ from the reference program's by a relative error of at most 0.025.
Values may be sent and summed in bfloat16 or wider, within the bound.
No kernel may reach another device: no remote copies, remote signals or barrier semaphores. Data moves between devices by JAX's collectives and lax.ppermute only.
A program may use at most 64 MiB of HBM per device.

```python
import jax
import jax.numpy as jnp
from jax import lax

D = 4096
HEAD_DIM = 256
HEADS = 16
MB = 4
TOK = 1024
S_ENC = 256
SECTIONS = 64
INNER = 4096


def plant(entries, stream_key, smallest, high):
    longest = entries.shape.index(max(entries.shape))
    spots = []
    for shift in (0, 1):
        where = [jax.random.randint(jax.random.fold_in(stream_key, axis), (), 0, length) for axis, length in enumerate(entries.shape)]
        where[longest] = (where[longest] + shift) % entries.shape[longest]
        spots.append(tuple(where))
    return entries.at[spots[0]].set(smallest).at[spots[1]].set(high)


def block_scale(stream_key, dims, shards, low, high):
    gain = 1.0
    for position, parts in shards:
        heights = jax.random.uniform(jax.random.fold_in(jax.random.fold_in(stream_key, 6), position), (parts,), jnp.float32, low / len(shards), high / len(shards))
        gain = gain * jnp.repeat(jnp.exp(heights), dims[position] // parts).reshape((-1,) + (1,) * (len(dims) - 1 - position))
    return gain


def gaussian(key, extent, scale, reach, cuts=(), kind=jnp.bfloat16):
    factor_of = block_scale(key, extent, cuts, -0.22, 0.18) if cuts else 1.0
    values = jax.random.normal(key, extent, jnp.float32) * scale * factor_of
    return jnp.minimum(jnp.maximum(values, -reach), reach).astype(kind)


def setup_inputs(seed: int = 0) -> dict:
    streams_of = jax.random.split(jax.random.key(seed), 7)
    return {
        "enc_out": gaussian(streams_of[0], (MB, S_ENC, D), 1.0, 6.0, ((1, 64),)),
        "kv_weight": gaussian(streams_of[1], (2, D, INNER), D ** -0.5, 0.09375, ((2, 16),)),
        "queries": gaussian(streams_of[2], (SECTIONS, TOK, INNER), 1.0, 6.0, ((0, 64), (2, 16))),
        "carried": gaussian(streams_of[3], (SECTIONS, TOK, INNER), 0.5, 4.0, ((0, 64), (2, 16))),
        "roster": plant(jax.random.randint(streams_of[4], (SECTIONS,), 0, MB), jax.random.fold_in(streams_of[4], 1), 0, MB - 1).astype(jnp.int32),
        "cotangent": gaussian(streams_of[5], (SECTIONS, TOK, INNER), 1.0, 6.0, ((0, 64), (2, 16))),
    }


def reference(enc_out, kv_weight, queries, carried, roster, cotangent):
    kv = jnp.einsum("msd,kdh->kmsh", enc_out.astype(jnp.float32), kv_weight.astype(jnp.float32)).astype(jnp.bfloat16)
    incoming_all = jnp.concatenate([jnp.zeros_like(carried[:1]), carried[:-1]], axis=0)
    micro_ids = jnp.arange(MB, dtype=jnp.int32)

    def one_section(total, items):
        query, incoming, grad_out, micro = items
        keys = lax.dynamic_index_in_dim(kv[0], micro, 0, keepdims=False).reshape(S_ENC, HEADS, HEAD_DIM).astype(jnp.float32)
        values = lax.dynamic_index_in_dim(kv[1], micro, 0, keepdims=False).reshape(S_ENC, HEADS, HEAD_DIM).astype(jnp.float32)
        qry = query.reshape(TOK, HEADS, HEAD_DIM).astype(jnp.float32)
        grad = grad_out.reshape(TOK, HEADS, HEAD_DIM).astype(jnp.float32)
        scores = jnp.einsum("thd,shd->hts", qry, keys) * 0.0625
        probs = jax.nn.softmax(scores, axis=-1)
        probs_low = probs.astype(jnp.bfloat16).astype(jnp.float32)
        context = jnp.einsum("hts,shd->thd", probs_low, values).reshape(TOK, HEADS * HEAD_DIM)
        result = (incoming.astype(jnp.float32) + context).astype(jnp.bfloat16)
        dprob = jnp.einsum("thd,shd->hts", grad, values)
        dscore = (probs * (dprob - jnp.sum(dprob * probs, axis=-1, keepdims=True)) * 0.0625).astype(jnp.bfloat16).astype(jnp.float32)
        dquery = jnp.einsum("hts,shd->thd", dscore, keys).reshape(TOK, HEADS * HEAD_DIM).astype(jnp.bfloat16)
        dkey = jnp.einsum("hts,thd->shd", dscore, qry).reshape(S_ENC, HEADS * HEAD_DIM)
        dvalue = jnp.einsum("hts,thd->shd", probs_low, grad).reshape(S_ENC, HEADS * HEAD_DIM)
        pick = (micro_ids == micro).astype(jnp.float32)[:, None, None]
        total = total + jnp.stack([pick * dkey[None], pick * dvalue[None]], axis=0)
        return total, (result, dquery)

    start = jnp.zeros((2, MB, S_ENC, HEADS * HEAD_DIM), jnp.float32)
    dkv, (section_out, d_queries) = lax.scan(one_section, start, (queries, incoming_all, cotangent, roster.astype(jnp.int32)))
    dkv_low = dkv.astype(jnp.bfloat16).astype(jnp.float32)
    d_enc_out = jnp.einsum("kmsh,kdh->msd", dkv_low, kv_weight.astype(jnp.float32)).astype(jnp.bfloat16)
    d_kv_weight = jnp.einsum("msd,kmsh->kdh", enc_out.astype(jnp.float32), dkv_low)
    return section_out, d_queries, d_enc_out, d_kv_weight
```

```python
import jax
import jax.numpy as jnp
from jax import lax
from jax.sharding import Mesh
from jax.sharding import PartitionSpec as P

HEAD_DIM = 256
SECTION = ("zl", "y", "core")
PLANE = ("y", "core")
HEADS = ("x", "zh")
BF = jnp.bfloat16
F32 = jnp.float32


def swap(value, axes):
    return lax.all_to_all(value, axes, split_axis=0, concat_axis=0, tiled=True)


def spread(value, axes):
    count = lax.axis_size(axes)
    return swap(jnp.broadcast_to(value[None], (count,) + value.shape), axes)


def dot(left, right, dims):
    return lax.dot_general(left, right, (dims, ((), ())), preferred_element_type=F32)


def per_device(enc_out, kv_weight, queries, carried, roster, cotangent):
    micros, held, width = enc_out.shape
    rows = micros * held
    planes = lax.axis_size("zl")
    mates = lax.axis_size(PLANE)
    xs = lax.axis_size("x")
    head = kv_weight.shape[2]
    tokens = queries.shape[1]
    enc_rows = enc_out.reshape(rows, width)

    names = spread(jnp.broadcast_to(roster[:, None], (8, 128)), PLANE)[:, 0, 0]

    kv = jnp.stack([dot(enc_rows, kv_weight[k], ((1,), (0,))) for k in range(2)]).astype(BF)
    kv_z = spread(kv.reshape(2 * rows, head), "zl")

    shape = (mates, 2, planes, held, planes, 2, micros, held)
    flat = (mates * 2 * planes * held, planes * 2 * micros * held)
    row = lax.broadcasted_iota(jnp.int32, flat, 0)
    col = lax.broadcasted_iota(jnp.int32, flat, 1)
    mate = row // (2 * planes * held)
    wanted = jnp.repeat(names, 2 * planes * held)[:, None]
    row_k, row_z, row_p = row // (planes * held) % 2, row // held % planes, row % held
    col_z, col_k, col_m, col_p = (
        col // (2 * micros * held),
        col // (micros * held) % 2,
        col // held % micros,
        col % held,
    )
    select = (
        (row_z == col_z) & (row_k == col_k) & (row_p == col_p) & (col_m == wanted)
    ).astype(BF)

    picked = dot(select, kv_z.reshape(flat[1], head), ((1,), (0,))).astype(BF)
    chosen = swap(picked.reshape(mates, 2 * planes * held, head), PLANE)
    chosen = chosen.reshape(mates, 2, planes * held, head)
    total = mates * planes * held
    keys = chosen[:, 0].reshape(total, head)
    values = chosen[:, 1].reshape(total, head)

    query, grad = queries[0], cotangent[0]
    scores = dot(query, keys, ((1,), (1,))) * 0.0625
    probs = jax.nn.softmax(scores, axis=-1)
    probs_low = probs.astype(BF)
    dprob = dot(grad, values, ((1,), (1,)))
    dscore = (probs * (dprob - jnp.sum(dprob * probs, axis=-1, keepdims=True)) * 0.0625).astype(BF)
    dkey = dot(dscore, query, ((0,), (0,))).astype(BF)
    dvalue = dot(probs_low, grad, ((0,), (0,))).astype(BF)
    share = jnp.stack(
        [dkey.reshape(mates, planes * held, head), dvalue.reshape(mates, planes * held, head)], axis=1
    )
    shared = swap(share.reshape(mates, 2 * planes * held, head), PLANE)
    plane_sum = dot(select, shared.reshape(flat[0], head), ((0,), (0,))).astype(BF)
    parts = swap(plane_sum.reshape(planes, 2 * rows, head), "zl")
    dkv = jnp.sum(parts.astype(F32), axis=0).astype(BF)

    dkv_k = dkv.reshape(2, rows, head)
    terms = dot(dkv_k[0], kv_weight[0], ((1,), (1,))) + dot(dkv_k[1], kv_weight[1], ((1,), (1,)))
    blocks = terms.astype(BF).reshape(rows, xs, width // xs).transpose(1, 0, 2)
    mine = jnp.sum(swap(blocks, "x").astype(F32), axis=0).astype(BF)
    mine = jnp.sum(spread(mine, "zh").astype(F32), axis=0).astype(BF)
    d_enc = spread(mine, "x").transpose(1, 0, 2).reshape(micros, held, width)

    enc_blocks = enc_rows.reshape(rows, planes, width // planes).transpose(1, 0, 2)
    enc_z = swap(enc_blocks, "zl").reshape(planes * rows, width // planes)
    dkv_z = spread(dkv, "zl").reshape(planes, 2, rows, head)
    partial = [
        dot(enc_z, dkv_z[:, k].reshape(planes * rows, head), ((0,), (0,)))
        .astype(BF)
        .reshape(mates, width // planes // mates, head)
        for k in range(2)
    ]
    pieces = swap(jnp.concatenate(partial, axis=1), PLANE)
    d_weight = jnp.sum(pieces.astype(F32), axis=0).reshape(2, width // planes // mates, head)

    count = lax.axis_size(SECTION)
    incoming = lax.ppermute(carried, SECTION, [(i, i + 1) for i in range(count - 1)])
    context = dot(probs_low, values, ((1,), (0,)))
    section_out = (incoming[0].astype(F32) + context).astype(BF)[None]
    d_queries = dot(dscore, keys, ((1,), (0,))).astype(BF)[None]
    return section_out, d_queries, d_enc, d_weight


def solution(mesh):
    inner = Mesh(mesh.devices.reshape(8, 4, 2, 4, 4), SECTION + HEADS)
    return jax.shard_map(
        per_device,
        mesh=inner,
        in_specs=(
            P(None, SECTION, None),
            P(None, None, HEADS),
            P(SECTION, None, HEADS),
            P(SECTION, None, HEADS),
            P(SECTION),
            P(SECTION, None, HEADS),
        ),
        out_specs=(
            P(SECTION, None, HEADS),
            P(SECTION, None, HEADS),
            P(None, SECTION, None),
            P(None, SECTION, HEADS),
        ),
        check_vma=False,
    )
```

```python
import jax
import jax.numpy as jnp
from jax import lax
from jax.sharding import Mesh
from jax.sharding import PartitionSpec as P

HEAD_DIM = 256
SECTION = ("zl", "y", "core")
PLANE = ("y", "core")
HEADS = ("x", "zh")
BF = jnp.bfloat16
F32 = jnp.float32


def swap(value, axes):
    return lax.all_to_all(value, axes, split_axis=0, concat_axis=0, tiled=True)


def spread(value, axes):
    count = lax.axis_size(axes)
    return swap(jnp.broadcast_to(value[None], (count,) + value.shape), axes)


def dot(left, right, dims):
    return lax.dot_general(left, right, (dims, ((), ())), preferred_element_type=F32)


def per_device(enc_out, kv_weight, queries, carried, roster, cotangent):
    micros, held, width = enc_out.shape
    rows = micros * held
    planes = lax.axis_size("zl")
    mates = lax.axis_size(PLANE)
    xs = lax.axis_size("x")
    zhs = lax.axis_size("zh")
    head = kv_weight.shape[2]
    tokens = queries.shape[1]
    enc_rows = enc_out.reshape(rows, width)

    names = spread(jnp.broadcast_to(roster[:, None], (8, 128)), PLANE)[:, 0, 0]

    kv = jnp.stack([dot(enc_rows, kv_weight[k], ((1,), (0,))) for k in range(2)]).astype(BF)
    kv_z = spread(kv.reshape(2 * rows, head), "zl")

    shape = (mates, 2, planes, held, planes, 2, micros, held)
    flat = (mates * 2 * planes * held, planes * 2 * micros * held)
    row = lax.broadcasted_iota(jnp.int32, flat, 0)
    col = lax.broadcasted_iota(jnp.int32, flat, 1)
    mate = row // (2 * planes * held)
    wanted = jnp.repeat(names, 2 * planes * held)[:, None]
    row_k, row_z, row_p = row // (planes * held) % 2, row // held % planes, row % held
    col_z, col_k, col_m, col_p = (
        col // (2 * micros * held),
        col // (micros * held) % 2,
        col // held % micros,
        col % held,
    )
    select = (
        (row_z == col_z) & (row_k == col_k) & (row_p == col_p) & (col_m == wanted)
    ).astype(BF)

    picked = dot(select, kv_z.reshape(flat[1], head), ((1,), (0,))).astype(BF)
    chosen = swap(picked.reshape(mates, 2 * planes * held, head), PLANE)
    chosen = chosen.reshape(mates, 2, planes * held, head)
    total = mates * planes * held
    keys = chosen[:, 0].reshape(total, head)
    values = chosen[:, 1].reshape(total, head)

    query, grad = queries[0], cotangent[0]
    scores = dot(query, keys, ((1,), (1,))) * 0.0625
    probs = jax.nn.softmax(scores, axis=-1)
    probs_low = probs.astype(BF)
    dprob = dot(grad, values, ((1,), (1,)))
    dscore = (probs * (dprob - jnp.sum(dprob * probs, axis=-1, keepdims=True)) * 0.0625).astype(BF)
    dkey = dot(dscore, query, ((0,), (0,))).astype(BF)
    dvalue = dot(probs_low, grad, ((0,), (0,))).astype(BF)
    share = jnp.stack(
        [dkey.reshape(mates, planes * held, head), dvalue.reshape(mates, planes * held, head)], axis=1
    )
    shared = swap(share.reshape(mates, 2 * planes * held, head), PLANE)
    plane_sum = dot(select, shared.reshape(flat[0], head), ((0,), (0,))).astype(BF)
    parts = swap(plane_sum.reshape(planes, 2 * rows, head), "zl")
    dkv = jnp.sum(parts.astype(F32), axis=0).astype(BF)

    count = lax.axis_size(SECTION)
    incoming = lax.ppermute(carried, SECTION, [(i, i + 1) for i in range(count - 1)])

    dkv_k = dkv.reshape(2, rows, head)
    terms = dot(dkv_k[0], kv_weight[0], ((1,), (1,))) + dot(dkv_k[1], kv_weight[1], ((1,), (1,)))
    blocks = terms.astype(BF).reshape(rows, xs, width // xs).transpose(1, 0, 2)
    mine = jnp.sum(swap(blocks, "x").astype(F32), axis=0).astype(BF)
    right = [(i, (i + 1) % zhs) for i in range(zhs)]
    left = [(i, (i - 1) % zhs) for i in range(zhs)]
    below = lax.ppermute(mine, "zh", right)
    above = lax.ppermute(mine, "zh", left)

    span = width // planes
    halves = span // head
    enc_blocks = enc_rows.reshape(rows, planes, halves, head).transpose(1, 2, 0, 3)
    enc_blocks = enc_blocks.reshape(planes, halves * rows, head)
    dkv, _ = lax.optimization_barrier((dkv, mine))
    sent = jnp.concatenate([enc_blocks, jnp.broadcast_to(dkv[None], (planes, 2 * rows, head))], axis=1)
    sent, incoming = lax.optimization_barrier((sent, incoming))
    got = swap(sent, "zl")

    context = dot(probs_low, values, ((1,), (0,)))
    section_out = (incoming[0].astype(F32) + context).astype(BF)[None]
    d_queries = dot(dscore, keys, ((1,), (0,))).astype(BF)[None]
    got, section_out, d_queries = lax.optimization_barrier((got, section_out, d_queries))

    got = got.reshape(planes, halves + 2, rows, head)
    column = [got[:, i].reshape(planes * rows, head) for i in range(halves + 2)]
    enc_z = jnp.concatenate(column[:halves], axis=1)
    dkv_z = jnp.concatenate(column[halves:], axis=1)
    partial = dot(enc_z, dkv_z, ((0,), (0,))).astype(BF)
    below, above, partial = lax.optimization_barrier((below, above, partial))
    half = rows // 2
    far = [lax.ppermute(below[:half], "zh", right), lax.ppermute(above[half:], "zh", left)]
    pieces = swap(partial.reshape(mates, span // mates, 2 * head), PLANE)
    *far, pieces = lax.optimization_barrier((*far, pieces))
    d_weight = jnp.sum(pieces.astype(F32), axis=0)
    d_weight = jnp.stack([d_weight[:, :head], d_weight[:, head:]])

    far = jnp.concatenate(far, axis=0)
    mine = (mine.astype(F32) + far.astype(F32)) + (below.astype(F32) + above.astype(F32))
    d_enc = spread(mine.astype(BF), "x").transpose(1, 0, 2).reshape(micros, held, width)

    return section_out, d_queries, d_enc, d_weight


def solution(mesh):
    inner = Mesh(mesh.devices.reshape(8, 4, 2, 4, 4), SECTION + HEADS)
    return jax.shard_map(
        per_device,
        mesh=inner,
        in_specs=(
            P(None, SECTION, None),
            P(None, None, HEADS),
            P(SECTION, None, HEADS),
            P(SECTION, None, HEADS),
            P(SECTION),
            P(SECTION, None, HEADS),
        ),
        out_specs=(
            P(SECTION, None, HEADS),
            P(SECTION, None, HEADS),
            P(None, SECTION, None),
            P(None, SECTION, HEADS),
        ),
        check_vma=False,
    )
```

```python
import jax
import jax.numpy as jnp
from jax import lax
from jax.experimental import pallas as pl
from jax.experimental.pallas import tpu as pltpu
from jax.sharding import Mesh
from jax.sharding import PartitionSpec as P

HEAD_DIM = 256
SECTION = ("zl", "y", "core")
PLANE = ("y", "core")
HEADS = ("x", "zh")
BF = jnp.bfloat16
F32 = jnp.float32


def swap(value, axes):
    return lax.all_to_all(value, axes, split_axis=0, concat_axis=0, tiled=True)


def spread(value, axes):
    count = lax.axis_size(axes)
    return swap(jnp.broadcast_to(value[None], (count,) + value.shape), axes)


def dot(left, right, dims):
    return lax.dot_general(left, right, (dims, ((), ())), preferred_element_type=F32)


CHUNKS = 4


def weight_copies(weight_ref, held, sems, places):
    span = held.shape[2]
    return [
        pltpu.make_async_copy(
            weight_ref.at[:, pl.ds(pl.multiple_of(place * span, span), span), :],
            held.at[chunk],
            sems.at[chunk],
        )
        for chunk, place in enumerate(places)
    ]


def project_kernel(enc_ref, weight_ref, out_ref, held, sems):
    copies = weight_copies(weight_ref, held, sems, range(CHUNKS))
    for copy in copies:
        copy.start()
    span = held.shape[2]
    total = [None, None]
    for chunk, copy in enumerate(copies):
        copy.wait()
        enc = enc_ref[:, chunk * span : (chunk + 1) * span]
        for k in range(2):
            part = dot(enc, held[chunk, k], ((1,), (0,)))
            total[k] = part if total[k] is None else total[k] + part
    for k in range(2):
        low = total[k].astype(BF)
        for at in range(out_ref.shape[0]):
            out_ref[at, k] = low


def project(enc_rows, kv_weight, copies):
    rows, width = enc_rows.shape
    head = kv_weight.shape[2]
    return pl.pallas_call(
        project_kernel,
        in_specs=[pl.BlockSpec(memory_space=pltpu.VMEM), pl.BlockSpec(memory_space=pltpu.HBM)],
        out_specs=pl.BlockSpec(memory_space=pltpu.VMEM),
        out_shape=jax.ShapeDtypeStruct((copies, 2, rows, head), BF),
        scratch_shapes=[
            pltpu.VMEM((CHUNKS, 2, width // CHUNKS, head), BF),
            pltpu.SemaphoreType.DMA((CHUNKS,)),
        ],
        compiler_params=pltpu.CompilerParams(vmem_limit_bytes=60 << 20),
    )(enc_rows, kv_weight)


def terms_kernel(place_ref, dkv_ref, weight_ref, out_ref, held, sems):
    blocks = out_ref.shape[0]
    places = [lax.rem(place_ref[0] + step, blocks) for step in range(blocks)]
    copies = weight_copies(weight_ref, held, sems, places)
    for copy in copies:
        copy.start()
    for step, copy in enumerate(copies):
        copy.wait()
        terms = dot(dkv_ref[0], held[step, 0], ((1,), (1,)))
        terms += dot(dkv_ref[1], held[step, 1], ((1,), (1,)))
        out_ref[step] = terms.astype(BF)


def encoder_terms(place, dkv, kv_weight, blocks):
    rows, head = dkv.shape[1:]
    span = kv_weight.shape[1] // blocks
    return pl.pallas_call(
        terms_kernel,
        in_specs=[
            pl.BlockSpec(memory_space=pltpu.SMEM),
            pl.BlockSpec(memory_space=pltpu.VMEM),
            pl.BlockSpec(memory_space=pltpu.HBM),
        ],
        out_specs=pl.BlockSpec(memory_space=pltpu.VMEM),
        out_shape=jax.ShapeDtypeStruct((blocks, rows, span), BF),
        scratch_shapes=[
            pltpu.VMEM((blocks, 2, span, head), BF),
            pltpu.SemaphoreType.DMA((blocks,)),
        ],
        compiler_params=pltpu.CompilerParams(vmem_limit_bytes=60 << 20),
    )(place, dkv, kv_weight)


def turned(value, axis, step):
    count = lax.axis_size(axis)
    return lax.ppermute(value, axis, [(i, (i + step) % count) for i in range(count)])


def per_device(enc_out, kv_weight, queries, carried, roster, cotangent):
    micros, held, width = enc_out.shape
    rows = micros * held
    planes = lax.axis_size("zl")
    mates = lax.axis_size(PLANE)
    xs = lax.axis_size("x")
    zhs = lax.axis_size("zh")
    head = kv_weight.shape[2]
    tokens = queries.shape[1]
    enc_rows = enc_out.reshape(rows, width)

    names = spread(jnp.broadcast_to(roster[:, None], (8, 128)), PLANE)[:, 0, 0]

    kv_z = swap(project(enc_rows, kv_weight, planes).reshape(planes, 2 * rows, head), "zl")

    shape = (mates, 2, planes, held, planes, 2, micros, held)
    flat = (mates * 2 * planes * held, planes * 2 * micros * held)
    row = lax.broadcasted_iota(jnp.int32, flat, 0)
    col = lax.broadcasted_iota(jnp.int32, flat, 1)
    mate = row // (2 * planes * held)
    wanted = jnp.repeat(names, 2 * planes * held)[:, None]
    row_k, row_z, row_p = row // (planes * held) % 2, row // held % planes, row % held
    col_z, col_k, col_m, col_p = (
        col // (2 * micros * held),
        col // (micros * held) % 2,
        col // held % micros,
        col % held,
    )
    select = (
        (row_z == col_z) & (row_k == col_k) & (row_p == col_p) & (col_m == wanted)
    ).astype(BF)

    picked = dot(select, kv_z.reshape(flat[1], head), ((1,), (0,))).astype(BF)
    chosen = swap(picked.reshape(mates, 2 * planes * held, head), PLANE)
    chosen = chosen.reshape(mates, 2, planes * held, head)
    total = mates * planes * held
    keys = chosen[:, 0].reshape(total, head)
    values = chosen[:, 1].reshape(total, head)

    query, grad = queries[0], cotangent[0]
    scores = dot(query, keys, ((1,), (1,))) * 0.0625
    probs = jax.nn.softmax(scores, axis=-1)
    probs_low = probs.astype(BF)
    dprob = dot(grad, values, ((1,), (1,)))
    dscore = (probs * (dprob - jnp.sum(dprob * probs, axis=-1, keepdims=True)) * 0.0625).astype(BF)
    dkey = dot(dscore, query, ((0,), (0,))).astype(BF)
    dvalue = dot(probs_low, grad, ((0,), (0,))).astype(BF)
    share = jnp.stack(
        [dkey.reshape(mates, planes * held, head), dvalue.reshape(mates, planes * held, head)], axis=1
    )
    shared = swap(share.reshape(mates, 2 * planes * held, head), PLANE)
    plane_sum = dot(select, shared.reshape(flat[0], head), ((0,), (0,))).astype(BF)
    parts = swap(plane_sum.reshape(planes, 2 * rows, head), "zl")
    dkv = jnp.sum(parts.astype(F32), axis=0).astype(BF)

    count = lax.axis_size(SECTION)
    incoming = lax.ppermute(carried, SECTION, [(i, i + 1) for i in range(count - 1)])

    span = width // planes
    halves = span // head
    enc_blocks = enc_rows.reshape(rows, planes, halves, head).transpose(1, 2, 0, 3)
    enc_blocks = enc_blocks.reshape(planes, halves * rows, head)
    sent = jnp.concatenate([enc_blocks, jnp.broadcast_to(dkv[None], (planes, 2 * rows, head))], axis=1)
    sent, incoming = lax.optimization_barrier((sent, incoming))
    got = swap(sent, "zl")

    place = lax.axis_index("x").astype(jnp.int32).reshape(1)
    terms = encoder_terms(place, dkv.reshape(2, rows, head), kv_weight, xs)
    sums = [turned(terms[step], "x", step) for step in range(1, xs)]
    mine = terms[0].astype(F32)
    for other in sums:
        mine = mine + other.astype(F32)
    got, mine = lax.optimization_barrier((got, mine.astype(BF)))
    ring = spread(mine, "zh")

    got = got.reshape(planes, halves + 2, rows, head)
    column = [got[:, i].reshape(planes * rows, head) for i in range(halves + 2)]
    enc_z = jnp.concatenate(column[:halves], axis=1)
    dkv_z = jnp.concatenate(column[halves:], axis=1)
    partial = dot(enc_z, dkv_z, ((0,), (0,))).astype(BF)
    ys, cores = lax.axis_size("y"), lax.axis_size("core")
    partial = partial.reshape(ys, cores, span // mates, 2 * head)
    core, y = lax.axis_index("core"), lax.axis_index("y")
    kept = lax.dynamic_index_in_dim(partial, core, 1, keepdims=False)
    given = lax.dynamic_index_in_dim(partial, 1 - core, 1, keepdims=False)
    pair = (kept.astype(F32) + turned(given, "core", 1).astype(F32)).astype(BF)
    d_weight = lax.dynamic_index_in_dim(pair, y, 0, keepdims=False).astype(F32)
    for step in range(1, ys):
        given = lax.dynamic_index_in_dim(pair, (y + step) % ys, 0, keepdims=False)
        d_weight = d_weight + turned(given, "y", step).astype(F32)
    d_weight = jnp.stack([d_weight[:, :head], d_weight[:, head:]])

    context = dot(probs_low, values, ((1,), (0,)))
    section_out = (incoming[0].astype(F32) + context).astype(BF)[None]
    d_queries = dot(dscore, keys, ((1,), (0,))).astype(BF)[None]

    ring, d_weight, section_out, d_queries = lax.optimization_barrier(
        (ring, d_weight, section_out, d_queries)
    )
    mine = jnp.sum(ring.astype(F32), axis=0).astype(BF)
    d_enc = spread(mine, "x").transpose(1, 0, 2).reshape(micros, held, width)
    return section_out, d_queries, d_enc, d_weight


def solution(mesh):
    inner = Mesh(mesh.devices.reshape(8, 4, 2, 4, 4), SECTION + HEADS)
    return jax.shard_map(
        per_device,
        mesh=inner,
        in_specs=(
            P(None, SECTION, None),
            P(None, None, HEADS),
            P(SECTION, None, HEADS),
            P(SECTION, None, HEADS),
            P(SECTION),
            P(SECTION, None, HEADS),
        ),
        out_specs=(
            P(SECTION, None, HEADS),
            P(SECTION, None, HEADS),
            P(None, SECTION, None),
            P(None, SECTION, HEADS),
        ),
        check_vma=False,
    )
```

```python
import jax
import jax.numpy as jnp
from jax import lax
from jax.sharding import Mesh
from jax.sharding import PartitionSpec as P

HEAD_DIM = 256
SECTION = ("zl", "y", "core")
PLANE = ("y", "core")
HEADS = ("x", "zh")
BF = jnp.bfloat16
F32 = jnp.float32


def swap(value, axes):
    return lax.all_to_all(value, axes, split_axis=0, concat_axis=0, tiled=True)


def spread(value, axes):
    count = lax.axis_size(axes)
    return swap(jnp.broadcast_to(value[None], (count,) + value.shape), axes)


def dot(left, right, dims):
    return lax.dot_general(left, right, (dims, ((), ())), preferred_element_type=F32)


def per_device(enc_out, kv_weight, queries, carried, roster, cotangent):
    micros, held, width = enc_out.shape
    rows = micros * held
    planes = lax.axis_size("zl")
    mates = lax.axis_size(PLANE)
    xs = lax.axis_size("x")
    zhs = lax.axis_size("zh")
    head = kv_weight.shape[2]
    tokens = queries.shape[1]
    enc_rows = enc_out.reshape(rows, width)

    names = spread(jnp.broadcast_to(roster[:, None], (8, 128)), PLANE)[:, 0, 0]

    kv = jnp.einsum("rd,kdh->krh", enc_rows, kv_weight, preferred_element_type=F32).astype(BF)
    kv_z = spread(kv.reshape(2 * rows, head), "zl")

    shape = (mates, 2, planes, held, planes, 2, micros, held)
    flat = (mates * 2 * planes * held, planes * 2 * micros * held)
    row = lax.broadcasted_iota(jnp.int32, flat, 0)
    col = lax.broadcasted_iota(jnp.int32, flat, 1)
    mate = row // (2 * planes * held)
    wanted = jnp.repeat(names, 2 * planes * held)[:, None]
    row_k, row_z, row_p = row // (planes * held) % 2, row // held % planes, row % held
    col_z, col_k, col_m, col_p = (
        col // (2 * micros * held),
        col // (micros * held) % 2,
        col // held % micros,
        col % held,
    )
    select = (
        (row_z == col_z) & (row_k == col_k) & (row_p == col_p) & (col_m == wanted)
    ).astype(BF)

    picked = dot(select, kv_z.reshape(flat[1], head), ((1,), (0,))).astype(BF)
    chosen = swap(picked.reshape(mates, 2 * planes * held, head), PLANE)
    chosen = chosen.reshape(mates, 2, planes * held, head)
    total = mates * planes * held
    keys = chosen[:, 0].reshape(total, head)
    values = chosen[:, 1].reshape(total, head)

    query, grad = queries[0], cotangent[0]
    scores = dot(query, keys, ((1,), (1,))) * 0.0625
    probs = jax.nn.softmax(scores, axis=-1)
    probs_low = probs.astype(BF)
    dprob = dot(grad, values, ((1,), (1,)))
    dscore = (probs * (dprob - jnp.sum(dprob * probs, axis=-1, keepdims=True)) * 0.0625).astype(BF)
    dkey = dot(dscore, query, ((0,), (0,))).astype(BF)
    dvalue = dot(probs_low, grad, ((0,), (0,))).astype(BF)
    share = jnp.stack(
        [dkey.reshape(mates, planes * held, head), dvalue.reshape(mates, planes * held, head)], axis=1
    )
    shared = swap(share.reshape(mates, 2 * planes * held, head), PLANE)
    plane_sum = dot(select, shared.reshape(flat[0], head), ((0,), (0,))).astype(BF)
    parts = swap(plane_sum.reshape(planes, 2 * rows, head), "zl")
    dkv = jnp.sum(parts.astype(F32), axis=0).astype(BF)

    count = lax.axis_size(SECTION)
    incoming = lax.ppermute(carried, SECTION, [(i, i + 1) for i in range(count - 1)])

    terms = jnp.einsum(
        "krh,kdh->rd", dkv.reshape(2, rows, head), kv_weight, preferred_element_type=F32
    )
    blocks = terms.astype(BF).reshape(rows, xs, width // xs).transpose(1, 0, 2)
    mine = jnp.sum(swap(blocks, "x").astype(F32), axis=0).astype(BF)
    pair = lax.ppermute(mine, "zh", [(i, i ^ 1) for i in range(zhs)])
    two = (mine.astype(F32) + pair.astype(F32)).astype(BF)

    context = dot(probs_low, values, ((1,), (0,)))
    section_out = (incoming[0].astype(F32) + context).astype(BF)[None]
    d_queries = dot(dscore, keys, ((1,), (0,))).astype(BF)[None]

    span = width // planes
    halves = span // head
    enc_blocks = enc_rows.reshape(rows, planes, halves, head).transpose(1, 2, 0, 3)
    enc_blocks = enc_blocks.reshape(planes, halves * rows, head)
    sent = jnp.concatenate([enc_blocks, jnp.broadcast_to(dkv[None], (planes, 2 * rows, head))], axis=1)
    sent, section_out, d_queries = lax.optimization_barrier((sent, section_out, d_queries))
    got = swap(sent, "zl")
    got = got.reshape(planes, halves + 2, rows, head)
    column = [got[:, i].reshape(planes * rows, head) for i in range(halves + 2)]
    enc_z = jnp.concatenate(column[:halves], axis=1)
    dkv_z = jnp.concatenate(column[halves:], axis=1)
    partial = dot(enc_z, dkv_z, ((0,), (0,))).astype(BF)
    two, partial = lax.optimization_barrier((two, partial))
    far = lax.ppermute(two, "zh", [(i, i ^ 2) for i in range(zhs)])
    pieces = swap(partial.reshape(mates, span // mates, 2 * head), PLANE)
    far, pieces = lax.optimization_barrier((far, pieces))
    d_weight = jnp.sum(pieces.astype(F32), axis=0)
    d_weight = jnp.stack([d_weight[:, :head], d_weight[:, head:]])
    mine = (two.astype(F32) + far.astype(F32)).astype(BF)
    d_enc = spread(mine, "x").transpose(1, 0, 2).reshape(micros, held, width)
    return section_out, d_queries, d_enc, d_weight


def solution(mesh):
    inner = Mesh(mesh.devices.reshape(8, 4, 2, 4, 4), SECTION + HEADS)
    return jax.shard_map(
        per_device,
        mesh=inner,
        in_specs=(
            P(None, SECTION, None),
            P(None, None, HEADS),
            P(SECTION, None, HEADS),
            P(SECTION, None, HEADS),
            P(SECTION),
            P(SECTION, None, HEADS),
        ),
        out_specs=(
            P(SECTION, None, HEADS),
            P(SECTION, None, HEADS),
            P(None, SECTION, None),
            P(None, SECTION, HEADS),
        ),
        check_vma=False,
    )
```

```python
import jax
import jax.numpy as jnp
from jax import lax
from jax.sharding import Mesh
from jax.sharding import PartitionSpec as P

HEAD_DIM = 256
SECTION = ("zl", "y", "core")
PLANE = ("y", "core")
HEADS = ("x", "zh")
BF = jnp.bfloat16
F32 = jnp.float32


def swap(value, axes):
    return lax.all_to_all(value, axes, split_axis=0, concat_axis=0, tiled=True)


def spread(value, axes):
    count = lax.axis_size(axes)
    return swap(jnp.broadcast_to(value[None], (count,) + value.shape), axes)


def dot(left, right, dims):
    return lax.dot_general(left, right, (dims, ((), ())), preferred_element_type=F32)


def turned(value, axis, step):
    count = lax.axis_size(axis)
    return lax.ppermute(value, axis, [(i, (i + step) % count) for i in range(count)])


def per_device(enc_out, kv_weight, queries, carried, roster, cotangent):
    micros, held, width = enc_out.shape
    rows = micros * held
    planes = lax.axis_size("zl")
    mates = lax.axis_size(PLANE)
    xs = lax.axis_size("x")
    head = kv_weight.shape[2]
    tokens = queries.shape[1]
    enc_rows = enc_out.reshape(rows, width)

    names = spread(jnp.broadcast_to(roster[:, None], (8, 128)), PLANE)[:, 0, 0]

    kv = jnp.einsum("rd,kdh->krh", enc_rows, kv_weight, preferred_element_type=F32).astype(BF)
    kv_z = spread(kv.reshape(2 * rows, head), "zl")

    shape = (mates, 2, planes, held, planes, 2, micros, held)
    flat = (mates * 2 * planes * held, planes * 2 * micros * held)
    row = lax.broadcasted_iota(jnp.int32, flat, 0)
    col = lax.broadcasted_iota(jnp.int32, flat, 1)
    mate = row // (2 * planes * held)
    wanted = jnp.repeat(names, 2 * planes * held)[:, None]
    row_k, row_z, row_p = row // (planes * held) % 2, row // held % planes, row % held
    col_z, col_k, col_m, col_p = (
        col // (2 * micros * held),
        col // (micros * held) % 2,
        col // held % micros,
        col % held,
    )
    select = (
        (row_z == col_z) & (row_k == col_k) & (row_p == col_p) & (col_m == wanted)
    ).astype(BF)

    picked = dot(select, kv_z.reshape(flat[1], head), ((1,), (0,))).astype(BF)
    chosen = swap(picked.reshape(mates, 2 * planes * held, head), PLANE)
    chosen = chosen.reshape(mates, 2, planes * held, head)
    total = mates * planes * held
    keys = chosen[:, 0].reshape(total, head)
    values = chosen[:, 1].reshape(total, head)

    query, grad = queries[0], cotangent[0]
    scores = dot(query, keys, ((1,), (1,))) * 0.0625
    probs = jax.nn.softmax(scores, axis=-1)
    probs_low = probs.astype(BF)
    dprob = dot(grad, values, ((1,), (1,)))
    dscore = (probs * (dprob - jnp.sum(dprob * probs, axis=-1, keepdims=True)) * 0.0625).astype(BF)
    dkey = dot(dscore, query, ((0,), (0,))).astype(BF)
    dvalue = dot(probs_low, grad, ((0,), (0,))).astype(BF)
    share = jnp.stack(
        [dkey.reshape(mates, planes * held, head), dvalue.reshape(mates, planes * held, head)], axis=1
    )
    shared = swap(share.reshape(mates, 2 * planes * held, head), PLANE)
    plane_sum = dot(select, shared.reshape(flat[0], head), ((0,), (0,))).astype(BF)
    parts = swap(plane_sum.reshape(planes, 2 * rows, head), "zl")
    dkv = jnp.sum(parts.astype(F32), axis=0).astype(BF)

    count = lax.axis_size(SECTION)
    incoming = lax.ppermute(carried, SECTION, [(i, i + 1) for i in range(count - 1)])

    span = width // planes
    halves = span // head
    enc_blocks = enc_rows.reshape(rows, planes, halves, head).transpose(1, 2, 0, 3)
    enc_blocks = enc_blocks.reshape(planes, halves * rows, head)
    sent = jnp.concatenate([enc_blocks, jnp.broadcast_to(dkv[None], (planes, 2 * rows, head))], axis=1)
    got = swap(sent, "zl")

    terms = jnp.einsum(
        "krh,kdh->rd", dkv.reshape(2, rows, head), kv_weight, preferred_element_type=F32
    )
    blocks = terms.astype(BF).reshape(rows, xs, width // xs).transpose(1, 0, 2)
    d_queries = dot(dscore, keys, ((1,), (0,))).astype(BF)[None]
    blocks, got, d_queries = lax.optimization_barrier((blocks, got, d_queries))
    mine = jnp.sum(swap(blocks, "x").astype(F32), axis=0).astype(BF)

    got = got.reshape(planes, halves + 2, rows, head)
    column = [got[:, i].reshape(planes * rows, head) for i in range(halves + 2)]
    enc_z = jnp.concatenate(column[:halves], axis=1)
    dkv_z = jnp.concatenate(column[halves:], axis=1)
    partial = dot(enc_z, dkv_z, ((0,), (0,))).astype(BF)
    ys, cores = lax.axis_size("y"), lax.axis_size("core")
    partial = partial.reshape(ys, cores, span // mates, 2 * head)
    core, y = lax.axis_index("core"), lax.axis_index("y")
    context = dot(probs_low, values, ((1,), (0,)))
    mine, partial, context, incoming = lax.optimization_barrier((mine, partial, context, incoming))
    ring = spread(mine, "zh")

    kept = lax.dynamic_index_in_dim(partial, core, 1, keepdims=False)
    given = lax.dynamic_index_in_dim(partial, 1 - core, 1, keepdims=False)
    pair = (kept.astype(F32) + turned(given, "core", 1).astype(F32)).astype(BF)
    d_weight = lax.dynamic_index_in_dim(pair, y, 0, keepdims=False).astype(F32)
    for step in range(1, ys):
        given = lax.dynamic_index_in_dim(pair, (y + step) % ys, 0, keepdims=False)
        d_weight = d_weight + turned(given, "y", step).astype(F32)
    d_weight = jnp.stack([d_weight[:, :head], d_weight[:, head:]])
    section_out = (incoming[0].astype(F32) + context).astype(BF)[None]
    ring, d_weight, section_out, d_queries = lax.optimization_barrier(
        (ring, d_weight, section_out, d_queries)
    )
    mine = jnp.sum(ring.astype(F32), axis=0).astype(BF)
    d_enc = spread(mine, "x").transpose(1, 0, 2).reshape(micros, held, width)
    return section_out, d_queries, d_enc, d_weight


def solution(mesh):
    inner = Mesh(mesh.devices.reshape(8, 4, 2, 4, 4), SECTION + HEADS)
    return jax.shard_map(
        per_device,
        mesh=inner,
        in_specs=(
            P(None, SECTION, None),
            P(None, None, HEADS),
            P(SECTION, None, HEADS),
            P(SECTION, None, HEADS),
            P(SECTION),
            P(SECTION, None, HEADS),
        ),
        out_specs=(
            P(SECTION, None, HEADS),
            P(SECTION, None, HEADS),
            P(None, SECTION, None),
            P(None, SECTION, HEADS),
        ),
        check_vma=False,
    )
```

```python
import jax
import jax.numpy as jnp
from jax import lax
from jax.sharding import Mesh
from jax.sharding import PartitionSpec as P

HEAD_DIM = 256
SECTION = ("zl", "y", "core")
PLANE = ("y", "core")
HEADS = ("x", "zh")
BF = jnp.bfloat16
F32 = jnp.float32


def swap(value, axes):
    return lax.all_to_all(value, axes, split_axis=0, concat_axis=0, tiled=True)


def spread(value, axes):
    count = lax.axis_size(axes)
    return swap(jnp.broadcast_to(value[None], (count,) + value.shape), axes)


def dot(left, right, dims):
    return lax.dot_general(left, right, (dims, ((), ())), preferred_element_type=F32)


def per_device(enc_out, kv_weight, queries, carried, roster, cotangent):
    micros, held, width = enc_out.shape
    rows = micros * held
    planes = lax.axis_size("zl")
    mates = lax.axis_size(PLANE)
    xs = lax.axis_size("x")
    zhs = lax.axis_size("zh")
    head = kv_weight.shape[2]
    tokens = queries.shape[1]
    enc_rows = enc_out.reshape(rows, width)

    names = spread(jnp.broadcast_to(roster[:, None], (1, 128)), PLANE)[:, 0, 0]

    kv = jnp.einsum("rd,kdh->krh", enc_rows, kv_weight, preferred_element_type=F32).astype(BF)
    kv_z = spread(kv.reshape(2 * rows, head), "zl")

    owned = planes * held
    flat = (mates * 2 * owned, planes * 2 * rows)
    selects = []
    for axis in range(2):
        extent = flat if axis == 0 else flat[::-1]
        row = lax.broadcasted_iota(jnp.int32, extent, axis)
        col = lax.broadcasted_iota(jnp.int32, extent, 1 - axis)
        wanted = jnp.expand_dims(jnp.repeat(names, 2 * owned), 1 - axis)
        match = (
            (row // held % planes == col // (2 * rows))
            & (row // owned % 2 == col // rows % 2)
            & (row % held == col % held)
            & (wanted == col // held % micros)
        )
        selects.append(match.astype(BF))
    select, unselect = lax.optimization_barrier(tuple(selects))

    picked = dot(select, kv_z.reshape(flat[1], head), ((1,), (0,))).astype(BF)
    chosen = swap(picked.reshape(mates, 2 * planes * held, head), PLANE)
    chosen = chosen.reshape(mates, 2, planes * held, head)
    total = mates * planes * held
    keys = chosen[:, 0].reshape(total, head)
    values = chosen[:, 1].reshape(total, head)

    query, grad = queries[0], cotangent[0]
    scores = dot(query, keys, ((1,), (1,))) * 0.0625
    probs = jax.nn.softmax(scores, axis=-1)
    probs_low = probs.astype(BF)
    dprob = dot(grad, values, ((1,), (1,)))
    dscore = (probs * (dprob - jnp.sum(dprob * probs, axis=-1, keepdims=True)) * 0.0625).astype(BF)
    dkey = dot(dscore, query, ((0,), (0,))).astype(BF)
    dvalue = dot(probs_low, grad, ((0,), (0,))).astype(BF)
    share = jnp.stack(
        [dkey.reshape(mates, planes * held, head), dvalue.reshape(mates, planes * held, head)], axis=1
    )
    shared = swap(share.reshape(mates, 2 * planes * held, head), PLANE)
    plane_sum = dot(unselect, shared.reshape(flat[0], head), ((1,), (0,))).astype(BF)
    parts = swap(plane_sum.reshape(planes, 2 * rows, head), "zl")
    dkv = jnp.sum(parts.astype(F32), axis=0).astype(BF)

    count = lax.axis_size(SECTION)
    incoming = lax.ppermute(carried, SECTION, [(i, i + 1) for i in range(count - 1)])

    context = dot(probs_low, values, ((1,), (0,)))
    d_queries = dot(dscore, keys, ((1,), (0,))).astype(BF)[None]
    dkv, context, d_queries = lax.optimization_barrier((dkv, context, d_queries))

    terms = jnp.einsum(
        "krh,kdh->rd", dkv.reshape(2, rows, head), kv_weight, preferred_element_type=F32
    )
    blocks = terms.astype(BF).reshape(rows, xs, width // xs).transpose(1, 0, 2)
    mine = jnp.sum(swap(blocks, "x").astype(F32), axis=0).astype(BF)
    pair = lax.ppermute(mine, "zh", [(i, i ^ 1) for i in range(zhs)])
    two = (mine.astype(F32) + pair.astype(F32)).astype(BF)

    span = width // planes
    halves = span // head
    enc_blocks = enc_rows.reshape(rows, planes, halves, head).transpose(1, 2, 0, 3)
    enc_blocks = enc_blocks.reshape(planes, halves * rows, head)
    sent = jnp.concatenate([enc_blocks, jnp.broadcast_to(dkv[None], (planes, 2 * rows, head))], axis=1)
    sent, mine, incoming = lax.optimization_barrier((sent, mine, incoming))
    got = swap(sent, "zl")
    got = got.reshape(planes, halves + 2, rows, head)
    column = [got[:, i].reshape(planes * rows, head) for i in range(halves + 2)]
    enc_z = jnp.concatenate(column[:halves], axis=1)
    dkv_z = jnp.concatenate(column[halves:], axis=1)
    partial = dot(enc_z, dkv_z, ((0,), (0,))).astype(BF)

    two, partial = lax.optimization_barrier((two, partial))
    far = lax.ppermute(two, "zh", [(i, i ^ 2) for i in range(zhs)])
    pieces = swap(partial.reshape(mates, span // mates, 2 * head), PLANE)
    far, pieces, incoming = lax.optimization_barrier((far, pieces, incoming))
    mine = (two.astype(F32) + far.astype(F32)).astype(BF)
    d_enc = spread(mine, "x").transpose(1, 0, 2).reshape(micros, held, width)

    d_weight = jnp.sum(pieces.astype(F32), axis=0)
    d_weight = jnp.stack([d_weight[:, :head], d_weight[:, head:]])
    section_out = (incoming[0].astype(F32) + context).astype(BF)[None]
    return section_out, d_queries, d_enc, d_weight


def solution(mesh):
    inner = Mesh(mesh.devices.reshape(8, 4, 2, 4, 4), SECTION + HEADS)
    return jax.shard_map(
        per_device,
        mesh=inner,
        in_specs=(
            P(None, SECTION, None),
            P(None, None, HEADS),
            P(SECTION, None, HEADS),
            P(SECTION, None, HEADS),
            P(SECTION),
            P(SECTION, None, HEADS),
        ),
        out_specs=(
            P(SECTION, None, HEADS),
            P(SECTION, None, HEADS),
            P(None, SECTION, None),
            P(None, SECTION, HEADS),
        ),
        check_vma=False,
    )
```

```python
import jax
import jax.numpy as jnp
from jax import lax
from jax.sharding import Mesh
from jax.sharding import PartitionSpec as P

HEAD_DIM = 256
SECTION = ("zl", "y", "core")
PLANE = ("y", "core")
HEADS = ("x", "zh")
BF = jnp.bfloat16
F32 = jnp.float32


def swap(value, axes):
    return lax.all_to_all(value, axes, split_axis=0, concat_axis=0, tiled=True)


def spread(value, axes):
    count = lax.axis_size(axes)
    return swap(jnp.broadcast_to(value[None], (count,) + value.shape), axes)


def dot(left, right, dims):
    return lax.dot_general(left, right, (dims, ((), ())), preferred_element_type=F32)


def per_device(enc_out, kv_weight, queries, carried, roster, cotangent):
    micros, held, width = enc_out.shape
    rows = micros * held
    planes = lax.axis_size("zl")
    mates = lax.axis_size(PLANE)
    xs = lax.axis_size("x")
    zhs = lax.axis_size("zh")
    head = kv_weight.shape[2]
    tokens = queries.shape[1]
    enc_rows = enc_out.reshape(rows, width)

    names = spread(jnp.broadcast_to(roster[:, None], (1, 128)), PLANE)[:, 0, 0]

    kv = jnp.einsum("rd,kdh->krh", enc_rows, kv_weight, preferred_element_type=F32).astype(BF)
    kv_z = spread(kv.reshape(2 * rows, head), "zl")

    owned = planes * held
    flat = (mates * 2 * owned, planes * 2 * rows)
    selects = []
    for axis in range(2):
        extent = flat if axis == 0 else flat[::-1]
        row = lax.broadcasted_iota(jnp.int32, extent, axis)
        col = lax.broadcasted_iota(jnp.int32, extent, 1 - axis)
        wanted = jnp.expand_dims(jnp.repeat(names, 2 * owned), 1 - axis)
        match = (
            (row // held % planes == col // (2 * rows))
            & (row // owned % 2 == col // rows % 2)
            & (row % held == col % held)
            & (wanted == col // held % micros)
        )
        selects.append(match.astype(BF))
    select, unselect = lax.optimization_barrier(tuple(selects))

    picked = dot(select, kv_z.reshape(flat[1], head), ((1,), (0,))).astype(BF)
    chosen = swap(picked.reshape(mates, 2 * planes * held, head), PLANE)
    chosen = chosen.reshape(mates, 2, planes * held, head)
    total = mates * planes * held
    keys = chosen[:, 0].reshape(total, head)
    values = chosen[:, 1].reshape(total, head)

    query, grad = queries[0], cotangent[0]
    scores = dot(query, keys, ((1,), (1,))) * 0.0625
    probs = jax.nn.softmax(scores, axis=-1)
    probs_low = probs.astype(BF)
    dprob = dot(grad, values, ((1,), (1,)))
    dscore = (probs * (dprob - jnp.sum(dprob * probs, axis=-1, keepdims=True)) * 0.0625).astype(BF)
    dkey = dot(dscore, query, ((0,), (0,))).astype(BF)
    dvalue = dot(probs_low, grad, ((0,), (0,))).astype(BF)
    share = jnp.stack(
        [dkey.reshape(mates, planes * held, head), dvalue.reshape(mates, planes * held, head)], axis=1
    )
    shared = swap(share.reshape(mates, 2 * planes * held, head), PLANE)
    plane_sum = dot(unselect, shared.reshape(flat[0], head), ((1,), (0,))).astype(BF)
    parts = swap(plane_sum.reshape(planes, 2 * rows, head), "zl")
    dkv = jnp.sum(parts.astype(F32), axis=0).astype(BF)

    count = lax.axis_size(SECTION)
    incoming = lax.ppermute(carried, SECTION, [(i, i + 1) for i in range(count - 1)])

    context = dot(probs_low, values, ((1,), (0,)))
    d_queries = dot(dscore, keys, ((1,), (0,))).astype(BF)[None]
    span = width // planes
    halves = span // head
    enc_blocks = enc_rows.reshape(rows, planes, halves, head).transpose(1, 2, 0, 3)
    enc_blocks = enc_blocks.reshape(planes, halves * rows, head)
    dkv, context, d_queries, enc_blocks = lax.optimization_barrier(
        (dkv, context, d_queries, enc_blocks)
    )

    terms = jnp.einsum(
        "krh,kdh->rd", dkv.reshape(2, rows, head), kv_weight, preferred_element_type=F32
    )
    blocks = terms.astype(BF).reshape(rows, xs, width // xs).transpose(1, 0, 2)
    mine = jnp.sum(swap(blocks, "x").astype(F32), axis=0).astype(BF)
    pair = lax.ppermute(mine, "zh", [(i, i ^ 1) for i in range(zhs)])
    two = (mine.astype(F32) + pair.astype(F32)).astype(BF)

    dkv, mine = lax.optimization_barrier((dkv, mine))
    sent = jnp.concatenate([enc_blocks, jnp.broadcast_to(dkv[None], (planes, 2 * rows, head))], axis=1)
    sent, mine, incoming = lax.optimization_barrier((sent, mine, incoming))
    got = swap(sent, "zl")
    got = got.reshape(planes, halves + 2, rows, head)
    column = [got[:, i].reshape(planes * rows, head) for i in range(halves + 2)]
    enc_z = jnp.concatenate(column[:halves], axis=1)
    dkv_z = jnp.concatenate(column[halves:], axis=1)
    partial = dot(enc_z, dkv_z, ((0,), (0,))).astype(BF)

    partial, _ = lax.optimization_barrier((partial, two))
    far = lax.ppermute(two, "zh", [(i, i ^ 2) for i in range(zhs)])
    pieces = swap(partial.reshape(mates, span // mates, 2 * head), PLANE)
    far, pieces, incoming = lax.optimization_barrier((far, pieces, incoming))
    mine = (two.astype(F32) + far.astype(F32)).astype(BF)
    d_enc = spread(mine.reshape(micros, held, width // xs), "x")
    d_enc = d_enc.transpose(1, 2, 0, 3).reshape(micros, held, width)

    d_weight = jnp.sum(pieces.astype(F32), axis=0)
    d_weight = jnp.stack([d_weight[:, :head], d_weight[:, head:]])
    section_out = (incoming[0].astype(F32) + context).astype(BF)[None]
    return section_out, d_queries, d_enc, d_weight


def solution(mesh):
    inner = Mesh(mesh.devices.reshape(8, 4, 2, 4, 4), SECTION + HEADS)
    return jax.shard_map(
        per_device,
        mesh=inner,
        in_specs=(
            P(None, SECTION, None),
            P(None, None, HEADS),
            P(SECTION, None, HEADS),
            P(SECTION, None, HEADS),
            P(SECTION),
            P(SECTION, None, HEADS),
        ),
        out_specs=(
            P(SECTION, None, HEADS),
            P(SECTION, None, HEADS),
            P(None, SECTION, None),
            P(None, SECTION, HEADS),
        ),
        check_vma=False,
    )
```

```python
import jax
import jax.numpy as jnp
from jax import lax
from jax.sharding import Mesh
from jax.sharding import PartitionSpec as P

HEAD_DIM = 256
SECTION = ("zl", "y", "core")
PLANE = ("y", "core")
HEADS = ("x", "zh")
BF = jnp.bfloat16
F32 = jnp.float32


def swap(value, axes):
    return lax.all_to_all(value, axes, split_axis=0, concat_axis=0, tiled=True)


def spread(value, axes):
    count = lax.axis_size(axes)
    return swap(jnp.broadcast_to(value[None], (count,) + value.shape), axes)


def dot(left, right, dims):
    return lax.dot_general(left, right, (dims, ((), ())), preferred_element_type=F32)


def per_device(enc_out, kv_weight, queries, carried, roster, cotangent):
    micros, held, width = enc_out.shape
    rows = micros * held
    planes = lax.axis_size("zl")
    mates = lax.axis_size(PLANE)
    xs = lax.axis_size("x")
    zhs = lax.axis_size("zh")
    head = kv_weight.shape[2]
    tokens = queries.shape[1]
    enc_rows = enc_out.reshape(rows, width)

    names = spread(jnp.broadcast_to(roster[:, None], (1, 128)), PLANE)[:, 0, 0]

    kv = jnp.einsum("rd,kdh->krh", enc_rows, kv_weight, preferred_element_type=F32).astype(BF)
    kv_z = spread(kv.reshape(2 * rows, head), "zl")

    owned = planes * held
    flat = (mates * 2 * owned, planes * 2 * rows)
    selects = []
    for axis in range(2):
        extent = flat if axis == 0 else flat[::-1]
        row = lax.broadcasted_iota(jnp.int32, extent, axis)
        col = lax.broadcasted_iota(jnp.int32, extent, 1 - axis)
        wanted = jnp.expand_dims(jnp.repeat(names, 2 * owned), 1 - axis)
        match = (
            (row // held % planes == col // (2 * rows))
            & (row // owned % 2 == col // rows % 2)
            & (row % held == col % held)
            & (wanted == col // held % micros)
        )
        selects.append(match.astype(BF))
    select, unselect = lax.optimization_barrier(tuple(selects))

    picked = dot(select, kv_z.reshape(flat[1], head), ((1,), (0,))).astype(BF)
    chosen = swap(picked.reshape(mates, 2 * planes * held, head), PLANE)
    chosen = chosen.reshape(mates, 2, planes * held, head)
    total = mates * planes * held
    keys = chosen[:, 0].reshape(total, head)
    values = chosen[:, 1].reshape(total, head)

    query, grad = queries[0], cotangent[0]
    scores = dot(query, keys, ((1,), (1,))) * 0.0625
    probs = jax.nn.softmax(scores, axis=-1)
    probs_low = probs.astype(BF)
    dprob = dot(grad, values, ((1,), (1,)))
    dscore = (probs * (dprob - jnp.sum(dprob * probs, axis=-1, keepdims=True)) * 0.0625).astype(BF)
    dkey = dot(dscore, query, ((0,), (0,))).astype(BF)
    dvalue = dot(probs_low, grad, ((0,), (0,))).astype(BF)
    share = jnp.stack(
        [dkey.reshape(mates, planes * held, head), dvalue.reshape(mates, planes * held, head)], axis=1
    )
    shared = swap(share.reshape(mates, 2 * planes * held, head), PLANE)
    plane_sum = dot(unselect, shared.reshape(flat[0], head), ((1,), (0,))).astype(BF)
    parts = swap(plane_sum.reshape(planes, 2 * rows, head), "zl")
    dkv = jnp.sum(parts.astype(F32), axis=0).astype(BF)

    count = lax.axis_size(SECTION)
    incoming = lax.ppermute(carried, SECTION, [(i, i + 1) for i in range(count - 1)])

    context = dot(probs_low, values, ((1,), (0,)))
    d_queries = dot(dscore, keys, ((1,), (0,))).astype(BF)[None]
    span = width // planes
    halves = span // head
    enc_blocks = enc_rows.reshape(rows, planes, halves, head).transpose(1, 2, 0, 3)
    enc_blocks = enc_blocks.reshape(planes, halves * rows, head)
    dkv, context, d_queries, enc_blocks = lax.optimization_barrier(
        (dkv, context, d_queries, enc_blocks)
    )

    terms = jnp.einsum(
        "krh,kdh->rd", dkv.reshape(2, rows, head), kv_weight, preferred_element_type=F32
    )
    blocks = terms.astype(BF).reshape(rows, xs, width // xs).transpose(1, 0, 2)
    mine = jnp.sum(swap(blocks, "x").astype(F32), axis=0).astype(BF)
    pair = lax.ppermute(mine, "zh", [(i, i ^ 1) for i in range(zhs)])
    two = (mine.astype(F32) + pair.astype(F32)).astype(BF)

    dkv, mine = lax.optimization_barrier((dkv, mine))
    sent = jnp.concatenate([enc_blocks, jnp.broadcast_to(dkv[None], (planes, 2 * rows, head))], axis=1)
    sent, mine, incoming = lax.optimization_barrier((sent, mine, incoming))
    got = swap(sent, "zl")
    got = got.reshape(planes, halves + 2, rows, head)
    column = [got[:, i].reshape(planes * rows, head) for i in range(halves + 2)]
    enc_z = jnp.concatenate(column[:halves], axis=1)
    dkv_z = jnp.concatenate(column[halves:], axis=1)
    partial = dot(enc_z, dkv_z, ((0,), (0,))).astype(BF)

    partial, _ = lax.optimization_barrier((partial, two))
    far = lax.ppermute(two, "zh", [(i, i ^ 2) for i in range(zhs)])
    pieces = swap(partial.reshape(mates, span // mates, 2 * head), PLANE)
    pieces, incoming = lax.optimization_barrier((pieces, incoming))
    section_out = (incoming[0].astype(F32) + context).astype(BF)[None]
    d_weight = jnp.sum(pieces.astype(F32), axis=0)
    d_weight = jnp.stack([d_weight[:, :head], d_weight[:, head:]])
    far, d_weight, section_out = lax.optimization_barrier((far, d_weight, section_out))
    mine = (two.astype(F32) + far.astype(F32)).astype(BF)
    d_enc = spread(mine.reshape(micros, held, width // xs), "x")
    d_enc = d_enc.transpose(1, 2, 0, 3).reshape(micros, held, width)
    return section_out, d_queries, d_enc, d_weight


def solution(mesh):
    inner = Mesh(mesh.devices.reshape(8, 4, 2, 4, 4), SECTION + HEADS)
    return jax.shard_map(
        per_device,
        mesh=inner,
        in_specs=(
            P(None, SECTION, None),
            P(None, None, HEADS),
            P(SECTION, None, HEADS),
            P(SECTION, None, HEADS),
            P(SECTION),
            P(SECTION, None, HEADS),
        ),
        out_specs=(
            P(SECTION, None, HEADS),
            P(SECTION, None, HEADS),
            P(None, SECTION, None),
            P(None, SECTION, HEADS),
        ),
        check_vma=False,
    )
```

```python
import jax
import jax.numpy as jnp
from jax import lax
from jax.sharding import Mesh
from jax.sharding import PartitionSpec as P

HEAD_DIM = 256
SECTION = ("zl", "y", "core")
PLANE = ("y", "core")
HEADS = ("x", "zh")
BF = jnp.bfloat16
F32 = jnp.float32


def swap(value, axes):
    return lax.all_to_all(value, axes, split_axis=0, concat_axis=0, tiled=True)


def spread(value, axes):
    count = lax.axis_size(axes)
    return swap(jnp.broadcast_to(value[None], (count,) + value.shape), axes)


def dot(left, right, dims):
    return lax.dot_general(left, right, (dims, ((), ())), preferred_element_type=F32)


def per_device(enc_out, kv_weight, queries, carried, roster, cotangent):
    micros, held, width = enc_out.shape
    rows = micros * held
    planes = lax.axis_size("zl")
    mates = lax.axis_size(PLANE)
    xs = lax.axis_size("x")
    zhs = lax.axis_size("zh")
    head = kv_weight.shape[2]
    tokens = queries.shape[1]
    enc_rows = enc_out.reshape(rows, width)

    names = spread(jnp.broadcast_to(roster[:, None], (1, 128)), PLANE)[:, 0, 0]

    kv = jnp.einsum("rd,kdh->krh", enc_rows, kv_weight, preferred_element_type=F32).astype(BF)
    kv_z = spread(kv.reshape(2 * rows, head), "zl")

    owned = planes * held
    flat = (mates * 2 * owned, planes * 2 * rows)
    selects = []
    for axis in range(2):
        extent = flat if axis == 0 else flat[::-1]
        row = lax.broadcasted_iota(jnp.int32, extent, axis)
        col = lax.broadcasted_iota(jnp.int32, extent, 1 - axis)
        wanted = jnp.expand_dims(jnp.repeat(names, 2 * owned), 1 - axis)
        match = (
            (row // held % planes == col // (2 * rows))
            & (row // owned % 2 == col // rows % 2)
            & (row % held == col % held)
            & (wanted == col // held % micros)
        )
        selects.append(match.astype(BF))
    select, unselect = lax.optimization_barrier(tuple(selects))

    picked = dot(select, kv_z.reshape(flat[1], head), ((1,), (0,))).astype(BF)
    chosen = swap(picked.reshape(mates, 2 * planes * held, head), PLANE)
    chosen = chosen.reshape(mates, 2, planes * held, head)
    total = mates * planes * held
    keys = chosen[:, 0].reshape(total, head)
    values = chosen[:, 1].reshape(total, head)

    query, grad = queries[0], cotangent[0]
    scores = dot(query, keys, ((1,), (1,))) * 0.0625
    probs = jax.nn.softmax(scores, axis=-1)
    probs_low = probs.astype(BF)
    dprob = dot(grad, values, ((1,), (1,)))
    dscore = (probs * (dprob - jnp.sum(dprob * probs, axis=-1, keepdims=True)) * 0.0625).astype(BF)
    dkey = dot(dscore, query, ((0,), (0,))).astype(BF)
    dvalue = dot(probs_low, grad, ((0,), (0,))).astype(BF)
    share = jnp.stack(
        [dkey.reshape(mates, planes * held, head), dvalue.reshape(mates, planes * held, head)], axis=1
    )
    shared = swap(share.reshape(mates, 2 * planes * held, head), PLANE)
    plane_sum = dot(unselect, shared.reshape(flat[0], head), ((1,), (0,))).astype(BF)
    parts = swap(plane_sum.reshape(planes, 2 * rows, head), "zl")
    dkv = jnp.sum(parts.astype(F32), axis=0).astype(BF)

    count = lax.axis_size(SECTION)
    incoming = lax.ppermute(carried, SECTION, [(i, i + 1) for i in range(count - 1)])

    span = width // planes
    halves = span // head
    enc_blocks = enc_rows.reshape(rows, planes, halves, head).transpose(1, 2, 0, 3)
    enc_blocks = enc_blocks.reshape(planes, halves * rows, head)
    dkv, enc_blocks = lax.optimization_barrier((dkv, enc_blocks))

    terms = jnp.einsum(
        "krh,kdh->rd", dkv.reshape(2, rows, head), kv_weight, preferred_element_type=F32
    )
    blocks = terms.astype(BF).reshape(rows, xs, width // xs).transpose(1, 0, 2)
    mine = jnp.sum(swap(blocks, "x").astype(F32), axis=0).astype(BF)
    pair = lax.ppermute(mine, "zh", [(i, i ^ 1) for i in range(zhs)])
    two = (mine.astype(F32) + pair.astype(F32)).astype(BF)

    dkv, mine = lax.optimization_barrier((dkv, mine))
    sent = jnp.concatenate([enc_blocks, jnp.broadcast_to(dkv[None], (planes, 2 * rows, head))], axis=1)
    sent, mine, incoming = lax.optimization_barrier((sent, mine, incoming))
    got = swap(sent, "zl")
    got = got.reshape(planes, halves + 2, rows, head)
    column = [got[:, i].reshape(planes * rows, head) for i in range(halves + 2)]
    enc_z = jnp.concatenate(column[:halves], axis=1)
    dkv_z = jnp.concatenate(column[halves:], axis=1)
    partial = dot(enc_z, dkv_z, ((0,), (0,))).astype(BF)

    partial, _ = lax.optimization_barrier((partial, two))
    far = lax.ppermute(two, "zh", [(i, i ^ 2) for i in range(zhs)])
    pieces = swap(partial.reshape(mates, span // mates, 2 * head), PLANE)
    pieces, incoming, probs_low, dscore = lax.optimization_barrier(
        (pieces, incoming, probs_low, dscore)
    )
    context = dot(probs_low, values, ((1,), (0,)))
    d_queries = dot(dscore, keys, ((1,), (0,))).astype(BF)[None]
    section_out = (incoming[0].astype(F32) + context).astype(BF)[None]
    d_weight = jnp.sum(pieces.astype(F32), axis=0)
    d_weight = jnp.stack([d_weight[:, :head], d_weight[:, head:]])
    far, d_weight, section_out, d_queries = lax.optimization_barrier(
        (far, d_weight, section_out, d_queries)
    )
    mine = (two.astype(F32) + far.astype(F32)).astype(BF)
    d_enc = spread(mine.reshape(micros, held, width // xs), "x")
    d_enc = d_enc.transpose(1, 2, 0, 3).reshape(micros, held, width)
    return section_out, d_queries, d_enc, d_weight


def solution(mesh):
    inner = Mesh(mesh.devices.reshape(8, 4, 2, 4, 4), SECTION + HEADS)
    return jax.shard_map(
        per_device,
        mesh=inner,
        in_specs=(
            P(None, SECTION, None),
            P(None, None, HEADS),
            P(SECTION, None, HEADS),
            P(SECTION, None, HEADS),
            P(SECTION),
            P(SECTION, None, HEADS),
        ),
        out_specs=(
            P(SECTION, None, HEADS),
            P(SECTION, None, HEADS),
            P(None, SECTION, None),
            P(None, SECTION, HEADS),
        ),
        check_vma=False,
    )
```
